32 devices in a mesh: row: 2 (over core), col: 4 (over y, x), layer: 4 (over z).
Axes of the slice: x: 2, y: 2, z: 4, core: 2. Of those that a mesh axis runs over, the one named last changes fastest.
Arguments:
- blocks: bfloat16 [128, 24, 128, 128], P(('row', 'col'), 'layer'), may hold values from -2 to 2
- pattern: int32 [128, 24], replicated, may hold values from 0 to 127, as said below
- out_pattern: int32 [128, 24], replicated, may hold values from 0 to 127, as said below
Outputs:
- product: bfloat16 [128, 24, 128, 128], P(('row', 'col'), 'layer')
The draws below stay inside these ranges and needn't reach their ends.
Inputs may be any that keep to these rules, and one draw needn't show every extreme that they name: `pattern`: block row i stores the block columns (i + d) mod 128 for 24 distinct offsets d from -12 to 12, always including 0, -12 and 12, in no particular order. `out_pattern`: the same law as pattern, drawn independently.
All inputs are finite; a program needn't handle non-finite values.
Results may differ from the reference program's by a relative error of at most 0.001.
Values may be sent and summed in bfloat16 or wider, within the bound.
A program may use at most 192 MiB of HBM per device.

```python
import jax
import jax.numpy as jnp
from jax import lax

BLOCK = 128
SLOTS = 24
REACH = 12
BLOCK_ROWS = 128


def band_pattern(key):
    inner = jnp.concatenate([jnp.arange(-REACH + 1, 0), jnp.arange(1, REACH)]).astype(jnp.int32)
    width = 2 * REACH - 2
    scores = jax.random.randint(jax.random.fold_in(key, 11), (BLOCK_ROWS, width), 0, 2 ** 20)
    scores = scores * width + jnp.arange(width, dtype=jnp.int32)[None, :]
    picks = jnp.argsort(scores, axis=1)[:, :SLOTS - 3]
    chosen = jnp.take(inner, picks)
    fixed = jnp.broadcast_to(jnp.array([0, -REACH, REACH], jnp.int32)[None, :], (BLOCK_ROWS, 3))
    offsets = jnp.concatenate([fixed, chosen], axis=1)
    order = jax.random.randint(jax.random.fold_in(key, 12), (BLOCK_ROWS, SLOTS), 0, 2 ** 20)
    order = order * SLOTS + jnp.arange(SLOTS, dtype=jnp.int32)[None, :]
    offsets = jnp.take_along_axis(offsets, jnp.argsort(order, axis=1), axis=1)
    rows = jnp.arange(BLOCK_ROWS, dtype=jnp.int32)[:, None]
    return ((rows + offsets) % BLOCK_ROWS).astype(jnp.int32)


def draw_pattern(key, part):
    return band_pattern(jax.random.fold_in(key, 1))


def draw_out_pattern(key, part):
    return band_pattern(jax.random.fold_in(key, 2))


def steps_of(own_key, dims, shards, smallest, top_value):
    level = 1.0
    for position, shards_of in shards:
        draws = jax.random.uniform(jax.random.fold_in(jax.random.fold_in(own_key, 6), position), (shards_of,), jnp.float32, smallest / len(shards), top_value / len(shards))
        level = level * jnp.repeat(jnp.exp(draws), dims[position] // shards_of).reshape((-1,) + (1,) * (len(dims) - 1 - position))
    return level


def scatter_about(stream_key, extent, scale, limit, split=(), held_as=jnp.bfloat16):
    values = jax.random.normal(stream_key, extent, jnp.float32) * scale
    if len(split) > 0:
        values = steps_of(stream_key, extent, split, -0.22, 0.18) * values
    return jnp.clip(values, min=-limit, max=limit).astype(held_as)


def setup_inputs(seed: int = 0) -> dict:
    arg_keys = jax.random.split(jax.random.key(seed), 4)
    blocks = scatter_about(arg_keys[0], (BLOCK_ROWS, SLOTS, BLOCK, BLOCK), 0.14, 2.0, ((0, 8), (1, 4)))
    pattern = draw_pattern(jax.random.fold_in(arg_keys[3], 71), 0)
    out_pattern = draw_out_pattern(jax.random.fold_in(arg_keys[3], 71), 0)
    return {"blocks": blocks, "pattern": pattern, "out_pattern": out_pattern}


def reference(blocks, pattern, out_pattern):
    def one_row(item):
        left, cols, out_cols = item
        right = jnp.take(blocks, cols, axis=0).astype(jnp.float32)
        right_cols = jnp.take(pattern, cols, axis=0)
        prods = jnp.einsum("tab,tubc->tuac", left.astype(jnp.float32), right, precision=lax.Precision.HIGHEST)
        match = (right_cols[:, :, None] == out_cols[None, None, :]).astype(jnp.int32)
        found = jnp.max(match, axis=-1)
        target = jnp.where(found > 0, jnp.argmax(match, axis=-1).astype(jnp.int32), jnp.int32(SLOTS)).astype(jnp.int32)
        sums = jax.ops.segment_sum(prods.reshape((SLOTS * SLOTS, BLOCK, BLOCK)), target.reshape(-1), num_segments=SLOTS + 1)
        return sums[:SLOTS]

    full = lax.map(one_row, (blocks, pattern, out_pattern))
    return full.astype(jnp.bfloat16)
```

```python
import functools

import jax
import jax.numpy as jnp
from jax import lax
from jax.experimental import pallas as pl
from jax.experimental.pallas import tpu as pltpu
from jax.sharding import PartitionSpec as P

REACH = 12
DIRECT = 6
MESH = pl.DeviceIdType.MESH


def gather_kernel(shape, blocks, full, local_sem, near_send, near_recv, far_send, far_recv, z_send, z_recv):
    rows_n, cols_n, layers = shape
    rows, slots = blocks.shape[:2]
    groups = rows_n * cols_n
    layer = lax.axis_index("layer")
    group = lax.axis_index("row") * cols_n + lax.axis_index("col")

    def at_group(g):
        return (lax.div(g, cols_n), lax.rem(g, cols_n), layer)

    right = at_group(lax.rem(group + 1, groups))
    left = at_group(lax.rem(group + groups - 1, groups))
    up = (lax.axis_index("row"), lax.axis_index("col"), lax.min(layer + 1, layers - 1))
    down = (lax.axis_index("row"), lax.axis_index("col"), lax.max(layer - 1, 0))
    has_up = layer < layers - 1
    has_down = layer > 0

    def own(first, count):
        return blocks.at[pl.ds(first, count)]

    def part(first, count, g):
        return full.at[pl.ds(first, count), pl.ds(g * slots, slots)]

    far = REACH - DIRECT
    half = rows // 2
    pieces = (
        (REACH, half),
        (REACH + half, rows - half),
        (REACH - DIRECT, DIRECT),
        (REACH + rows, DIRECT),
    )

    barrier = pltpu.get_barrier_semaphore()
    for other in (left, right):
        pl.semaphore_signal(barrier, inc=1, device_id=other, device_id_type=MESH)

    @pl.when(has_up)
    def _():
        pl.semaphore_signal(barrier, inc=1, device_id=up, device_id_type=MESH)

    @pl.when(has_down)
    def _():
        pl.semaphore_signal(barrier, inc=1, device_id=down, device_id_type=MESH)

    pl.semaphore_wait(barrier, 2 + has_up.astype(jnp.int32) + has_down.astype(jnp.int32))

    def remote(src, dst, send, recv, target):
        return pltpu.make_async_remote_copy(
            src_ref=src, dst_ref=dst, send_sem=send, recv_sem=recv, device_id=target, device_id_type=MESH
        )

    keep = pltpu.make_async_copy(blocks, part(REACH, rows, layer), local_sem)
    keep.start()

    near_right = remote(own(rows - DIRECT, DIRECT), part(REACH - DIRECT, DIRECT, layer), near_send.at[0], near_recv.at[0], right)
    near_left = remote(own(0, DIRECT), part(REACH + rows, DIRECT, layer), near_send.at[1], near_recv.at[1], left)
    near_right.start()
    near_left.start()

    def along(p, g, direction, src=None):
        first, count = pieces[p]
        return remote(
            part(first, count, g) if src is None else src,
            part(first, count, g),
            z_send.at[p, direction, g],
            z_recv.at[p, g],
            up if direction == 0 else down,
        )

    def start_along(p, g, direction, src=None):
        @pl.when(has_up if direction == 0 else has_down)
        def _():
            along(p, g, direction, src).start()

    for p in (0, 1):
        src = own(pieces[p][0] - REACH, pieces[p][1])
        start_along(p, layer, 0, src)
        start_along(p, layer, 1, src)

    def far_copies(g, from_blocks=False):
        def of(first):
            return own(first, far) if from_blocks else part(REACH + first, far, g)

        to_right = remote(of(rows - REACH), part(0, far, g), far_send.at[0, g], far_recv.at[0, g], right)
        to_left = remote(of(DIRECT), part(REACH + rows + DIRECT, far, g), far_send.at[1, g], far_recv.at[1, g], left)
        return to_right, to_left

    for copy in far_copies(layer, True):
        copy.start()

    def forward(p, hop):
        @pl.when(layer >= hop)
        def _():
            g = layer - hop
            along(p, g, 0).wait_recv()
            start_along(p, g, 0)

        @pl.when(layer + hop < layers)
        def _():
            g = layer + hop
            along(p, g, 1).wait_recv()
            start_along(p, g, 1)

    def start_far(hop):
        @pl.when(layer >= hop)
        def _():
            for copy in far_copies(layer - hop):
                copy.start()

        @pl.when(layer + hop < layers)
        def _():
            for copy in far_copies(layer + hop):
                copy.start()

    for hop in range(1, layers):
        forward(0, hop)
        forward(1, hop)
        start_far(hop)
        if hop == 1:
            near_right.wait_recv()
            start_along(2, layer, 0)
            start_along(2, layer, 1)
            near_left.wait_recv()
            start_along(3, layer, 0)
            start_along(3, layer, 1)
        else:
            forward(2, hop - 1)
            forward(3, hop - 1)
    if layers == 1:
        near_right.wait_recv()
        near_left.wait_recv()
    else:
        forward(2, layers - 1)
        forward(3, layers - 1)

    for g in range(layers):
        for copy in far_copies(g):
            copy.wait()
    near_right.wait_send()
    near_left.wait_send()
    for p in range(4):
        for g in range(layers):
            @pl.when(has_up & (layer >= g))
            def _():
                along(p, g, 0).wait_send()

            @pl.when(has_down & (layer <= g))
            def _():
                along(p, g, 1).wait_send()

    keep.wait()


def gather_rows(blocks, shape):
    rows, slots = blocks.shape[:2]
    layers = shape[2]
    return pl.pallas_call(
        functools.partial(gather_kernel, shape),
        out_shape=jax.ShapeDtypeStruct((rows + 2 * REACH, slots * layers) + blocks.shape[2:], blocks.dtype),
        in_specs=[pl.BlockSpec(memory_space=pl.ANY)],
        out_specs=pl.BlockSpec(memory_space=pl.ANY),
        scratch_shapes=[
            pltpu.SemaphoreType.DMA,
            pltpu.SemaphoreType.DMA((2,)),
            pltpu.SemaphoreType.DMA((2,)),
            pltpu.SemaphoreType.DMA((2, layers)),
            pltpu.SemaphoreType.DMA((2, layers)),
            pltpu.SemaphoreType.DMA((4, 2, layers)),
            pltpu.SemaphoreType.DMA((4, layers)),
        ],
        compiler_params=pltpu.CompilerParams(collective_id=0, has_side_effects=True),
    )(blocks)


def multiply_kernel(picked, full, out, held, sems):
    row = pl.program_id(0)
    outer, slots = full.shape[:2]
    wanted = out.shape[1]

    def fetch(r):
        return pltpu.make_async_copy(full.at[r], held.at[pl.ds(r * slots, slots)], sems.at[r])

    @pl.when(row == 0)
    def _():
        @pl.loop(0, outer)
        def _(r):
            fetch(r).start()

        held[outer * slots] = jnp.zeros(held.shape[1:], held.dtype)

        @pl.loop(0, 2 * REACH)
        def _(r):
            fetch(r).wait()

    fetch(row + 2 * REACH).wait()

    mine = (row + REACH) * slots
    lhs = jnp.concatenate([held[mine + t] for t in range(slots)], axis=1)
    for s in range(0, wanted, 2):
        pair = range(s, min(s + 2, wanted))
        rhs = jnp.concatenate(
            [
                jnp.concatenate([held[picked[row, k * slots + t]] for k in pair], axis=1)
                for t in range(slots)
            ],
            axis=0,
        )
        sums = jnp.dot(lhs, rhs, preferred_element_type=jnp.float32).astype(out.dtype)
        for n, k in enumerate(pair):
            out[0, k] = sums[:, n * out.shape[3] : (n + 1) * out.shape[3]]


def multiply(full, picked, rows, wanted):
    outer, slots, size = full.shape[:3]
    return pl.pallas_call(
        multiply_kernel,
        out_shape=jax.ShapeDtypeStruct((rows, wanted, size, size), full.dtype),
        grid_spec=pltpu.PrefetchScalarGridSpec(
            num_scalar_prefetch=1,
            grid=(rows,),
            in_specs=[pl.BlockSpec(memory_space=pl.ANY)],
            out_specs=pl.BlockSpec((1, wanted, size, size), lambda i, picked: (i, 0, 0, 0)),
            scratch_shapes=[
                pltpu.VMEM((outer * slots + 1, size, size), full.dtype),
                pltpu.SemaphoreType.DMA((outer,)),
            ],
        ),
        compiler_params=pltpu.CompilerParams(
            dimension_semantics=("arbitrary",), vmem_limit_bytes=48 * 2**20
        ),
    )(picked, full)


def per_device(shape, blocks, pattern, out_pattern):
    rows, wanted = blocks.shape[:2]
    total, slots = pattern.shape
    outer = rows + 2 * REACH
    first = lax.axis_index(("row", "col")) * rows
    full = gather_rows(blocks, shape)
    own_cols = lax.dynamic_slice_in_dim(pattern, first, rows, 0)
    own_out = lax.dynamic_slice(out_pattern, (first, lax.axis_index("layer") * wanted), (rows, wanted))
    where = (own_cols - (first - REACH)) % total
    right_cols = jnp.take(pattern, own_cols, axis=0)
    match = right_cols[:, None, :, :] == own_out[:, :, None, None]
    slot = jnp.max(jnp.where(match, jnp.arange(1, slots + 1, dtype=jnp.int32), 0), axis=-1)
    picked = jnp.where(slot > 0, where[:, None, :] * slots + slot - 1, outer * slots)
    return multiply(full, picked.reshape(rows, wanted * slots), rows, wanted)


def solution(mesh):
    shape = tuple(mesh.shape[axis] for axis in ("row", "col", "layer"))
    spec = P(("row", "col"), "layer", None, None)
    return jax.shard_map(
        functools.partial(per_device, shape),
        mesh=mesh,
        in_specs=(spec, P(), P()),
        out_specs=spec,
        check_vma=False,
    )
```

```python
import functools

import jax
import jax.numpy as jnp
from jax import lax
from jax.experimental import pallas as pl
from jax.experimental.pallas import tpu as pltpu
from jax.sharding import PartitionSpec as P

REACH = 12
DIRECT = 4
MESH = pl.DeviceIdType.MESH


def gather_kernel(shape, blocks, full, local_sem, near_send, near_recv, far_send, far_recv, z_send, z_recv):
    rows_n, cols_n, layers = shape
    rows, slots = blocks.shape[:2]
    groups = rows_n * cols_n
    layer = lax.axis_index("layer")
    group = lax.axis_index("row") * cols_n + lax.axis_index("col")

    def at_group(g):
        return (lax.div(g, cols_n), lax.rem(g, cols_n), layer)

    right = at_group(lax.rem(group + 1, groups))
    left = at_group(lax.rem(group + groups - 1, groups))
    up = (lax.axis_index("row"), lax.axis_index("col"), lax.min(layer + 1, layers - 1))
    down = (lax.axis_index("row"), lax.axis_index("col"), lax.max(layer - 1, 0))
    has_up = layer < layers - 1
    has_down = layer > 0

    def own(first, count):
        return blocks.at[pl.ds(first, count)]

    def part(first, count, g):
        return full.at[pl.ds(first, count), pl.ds(g * slots, slots)]

    far = REACH - DIRECT
    half = rows // 2
    pieces = (
        (REACH, half),
        (REACH + half, rows - half),
        (REACH - DIRECT, DIRECT),
        (REACH + rows, DIRECT),
    )

    barrier = pltpu.get_barrier_semaphore()
    for other in (left, right):
        pl.semaphore_signal(barrier, inc=1, device_id=other, device_id_type=MESH)

    @pl.when(has_up)
    def _():
        pl.semaphore_signal(barrier, inc=1, device_id=up, device_id_type=MESH)

    @pl.when(has_down)
    def _():
        pl.semaphore_signal(barrier, inc=1, device_id=down, device_id_type=MESH)

    pl.semaphore_wait(barrier, 2 + has_up.astype(jnp.int32) + has_down.astype(jnp.int32))

    def remote(src, dst, send, recv, target):
        return pltpu.make_async_remote_copy(
            src_ref=src, dst_ref=dst, send_sem=send, recv_sem=recv, device_id=target, device_id_type=MESH
        )

    keep = pltpu.make_async_copy(blocks, part(REACH, rows, layer), local_sem)
    keep.start()

    near_right = remote(own(rows - DIRECT, DIRECT), part(REACH - DIRECT, DIRECT, layer), near_send.at[0], near_recv.at[0], right)
    near_left = remote(own(0, DIRECT), part(REACH + rows, DIRECT, layer), near_send.at[1], near_recv.at[1], left)
    near_right.start()
    near_left.start()

    def along(p, g, direction, src=None):
        first, count = pieces[p]
        return remote(
            part(first, count, g) if src is None else src,
            part(first, count, g),
            z_send.at[p, direction, g],
            z_recv.at[p, g],
            up if direction == 0 else down,
        )

    def start_along(p, g, direction, src=None):
        @pl.when(has_up if direction == 0 else has_down)
        def _():
            along(p, g, direction, src).start()

    for p in (0, 1):
        src = own(pieces[p][0] - REACH, pieces[p][1])
        start_along(p, layer, 0, src)
        start_along(p, layer, 1, src)

    def far_copies(g, from_blocks=False):
        def of(first):
            return own(first, far) if from_blocks else part(REACH + first, far, g)

        to_right = remote(of(rows - REACH), part(0, far, g), far_send.at[0, g], far_recv.at[0, g], right)
        to_left = remote(of(DIRECT), part(REACH + rows + DIRECT, far, g), far_send.at[1, g], far_recv.at[1, g], left)
        return to_right, to_left

    for copy in far_copies(layer, True):
        copy.start()

    def forward(p, hop):
        @pl.when(layer >= hop)
        def _():
            g = layer - hop
            along(p, g, 0).wait_recv()
            start_along(p, g, 0)

        @pl.when(layer + hop < layers)
        def _():
            g = layer + hop
            along(p, g, 1).wait_recv()
            start_along(p, g, 1)

    def start_far(hop):
        @pl.when(layer >= hop)
        def _():
            for copy in far_copies(layer - hop):
                copy.start()

        @pl.when(layer + hop < layers)
        def _():
            for copy in far_copies(layer + hop):
                copy.start()

    for hop in range(1, layers):
        forward(0, hop)
        forward(1, hop)
        start_far(hop)
        if hop == 1:
            near_right.wait_recv()
            start_along(2, layer, 0)
            start_along(2, layer, 1)
            near_left.wait_recv()
            start_along(3, layer, 0)
            start_along(3, layer, 1)
        else:
            forward(2, hop - 1)
            forward(3, hop - 1)
    if layers == 1:
        near_right.wait_recv()
        near_left.wait_recv()
    else:
        forward(2, layers - 1)
        forward(3, layers - 1)

    for g in range(layers):
        for copy in far_copies(g):
            copy.wait()
    near_right.wait_send()
    near_left.wait_send()
    for p in range(4):
        for g in range(layers):
            @pl.when(has_up & (layer >= g))
            def _():
                along(p, g, 0).wait_send()

            @pl.when(has_down & (layer <= g))
            def _():
                along(p, g, 1).wait_send()

    keep.wait()


def gather_rows(blocks, shape):
    rows, slots = blocks.shape[:2]
    layers = shape[2]
    return pl.pallas_call(
        functools.partial(gather_kernel, shape),
        out_shape=jax.ShapeDtypeStruct((rows + 2 * REACH, slots * layers) + blocks.shape[2:], blocks.dtype),
        in_specs=[pl.BlockSpec(memory_space=pl.ANY)],
        out_specs=pl.BlockSpec(memory_space=pl.ANY),
        scratch_shapes=[
            pltpu.SemaphoreType.DMA,
            pltpu.SemaphoreType.DMA((2,)),
            pltpu.SemaphoreType.DMA((2,)),
            pltpu.SemaphoreType.DMA((2, layers)),
            pltpu.SemaphoreType.DMA((2, layers)),
            pltpu.SemaphoreType.DMA((4, 2, layers)),
            pltpu.SemaphoreType.DMA((4, layers)),
        ],
        compiler_params=pltpu.CompilerParams(collective_id=0, has_side_effects=True),
    )(blocks)


def multiply_kernel(picked, full, out, held, sems):
    row = pl.program_id(0)
    outer, slots = full.shape[:2]
    wanted = out.shape[1]

    def fetch(r):
        return pltpu.make_async_copy(full.at[r], held.at[pl.ds(r * slots, slots)], sems.at[r])

    @pl.when(row == 0)
    def _():
        @pl.loop(0, outer)
        def _(r):
            fetch(r).start()

        held[outer * slots] = jnp.zeros(held.shape[1:], held.dtype)

        @pl.loop(0, 2 * REACH)
        def _(r):
            fetch(r).wait()

    fetch(row + 2 * REACH).wait()

    mine = (row + REACH) * slots
    lhs = jnp.concatenate([held[mine + t] for t in range(slots)], axis=1)
    for s in range(0, wanted, 2):
        pair = range(s, min(s + 2, wanted))
        rhs = jnp.concatenate(
            [
                jnp.concatenate([held[picked[row, k * slots + t]] for k in pair], axis=1)
                for t in range(slots)
            ],
            axis=0,
        )
        sums = jnp.dot(lhs, rhs, preferred_element_type=jnp.float32).astype(out.dtype)
        for n, k in enumerate(pair):
            out[0, k] = sums[:, n * out.shape[3] : (n + 1) * out.shape[3]]


def multiply(full, picked, rows, wanted):
    outer, slots, size = full.shape[:3]
    return pl.pallas_call(
        multiply_kernel,
        out_shape=jax.ShapeDtypeStruct((rows, wanted, size, size), full.dtype),
        grid_spec=pltpu.PrefetchScalarGridSpec(
            num_scalar_prefetch=1,
            grid=(rows,),
            in_specs=[pl.BlockSpec(memory_space=pl.ANY)],
            out_specs=pl.BlockSpec((1, wanted, size, size), lambda i, picked: (i, 0, 0, 0)),
            scratch_shapes=[
                pltpu.VMEM((outer * slots + 1, size, size), full.dtype),
                pltpu.SemaphoreType.DMA((outer,)),
            ],
        ),
        compiler_params=pltpu.CompilerParams(
            dimension_semantics=("arbitrary",), vmem_limit_bytes=48 * 2**20
        ),
    )(picked, full)


def per_device(shape, blocks, pattern, out_pattern):
    rows, wanted = blocks.shape[:2]
    total, slots = pattern.shape
    outer = rows + 2 * REACH
    first = lax.axis_index(("row", "col")) * rows
    full = gather_rows(blocks, shape)
    own_cols = lax.dynamic_slice_in_dim(pattern, first, rows, 0)
    own_out = lax.dynamic_slice(out_pattern, (first, lax.axis_index("layer") * wanted), (rows, wanted))
    where = (own_cols - (first - REACH)) % total
    right_cols = jnp.take(pattern, own_cols, axis=0)
    match = right_cols[:, None, :, :] == own_out[:, :, None, None]
    slot = jnp.max(jnp.where(match, jnp.arange(1, slots + 1, dtype=jnp.int32), 0), axis=-1)
    picked = jnp.where(slot > 0, where[:, None, :] * slots + slot - 1, outer * slots)
    return multiply(full, picked.reshape(rows, wanted * slots), rows, wanted)


def solution(mesh):
    shape = tuple(mesh.shape[axis] for axis in ("row", "col", "layer"))
    spec = P(("row", "col"), "layer", None, None)
    return jax.shard_map(
        functools.partial(per_device, shape),
        mesh=mesh,
        in_specs=(spec, P(), P()),
        out_specs=spec,
        check_vma=False,
    )
```

```python
import functools

import jax
import jax.numpy as jnp
from jax import lax
from jax.experimental import pallas as pl
from jax.experimental.pallas import tpu as pltpu
from jax.sharding import PartitionSpec as P

REACH = 12
DIRECT = 1
PIECES = 8
MESH = pl.DeviceIdType.MESH


def gather_kernel(shape, blocks, full, local_sem, near_send, near_recv, far_send, far_recv, on_send, on_recv, z_send, z_recv):
    rows_n, cols_n, layers = shape
    rows, slots = blocks.shape[:2]
    groups = rows_n * cols_n
    row, col, layer = (lax.axis_index(axis) for axis in ("row", "col", "layer"))
    group = row * cols_n + col
    odd = lax.rem(group, 2)

    def at_group(g):
        g = lax.rem(g + groups, groups)
        return (lax.div(g, cols_n), lax.rem(g, cols_n), layer)

    right, left = at_group(group + 1), at_group(group - 1)
    partner = at_group(group + 1 - 2 * odd)
    beyond = at_group(group + 2 - 4 * odd)
    behind = at_group(group - 2 + 4 * odd)
    up = (row, col, lax.min(layer + 1, layers - 1))
    down = (row, col, lax.max(layer - 1, 0))
    has_up = layer < layers - 1
    has_down = layer > 0

    step = rows // PIECES
    pieces = tuple((rows + k * step, step) for k in range(PIECES)) + (
        (rows - DIRECT, DIRECT),
        (2 * rows, DIRECT),
    )
    before, after = (DIRECT, REACH), (rows - REACH, rows - DIRECT)

    def cut(k, low, high):
        first, last = max(k * step, low), min((k + 1) * step, high)
        return first, max(last - first, 0)

    def own(first, count):
        return blocks.at[pl.ds(first, count)]

    def part(first, count, g):
        return full.at[pl.ds(first, count), pl.ds(g * slots, slots)]

    barrier = pltpu.get_barrier_semaphore()
    for other in (left, right, beyond, behind):
        pl.semaphore_signal(barrier, inc=1, device_id=other, device_id_type=MESH)

    @pl.when(has_up)
    def _():
        pl.semaphore_signal(barrier, inc=1, device_id=up, device_id_type=MESH)

    @pl.when(has_down)
    def _():
        pl.semaphore_signal(barrier, inc=1, device_id=down, device_id_type=MESH)

    pl.semaphore_wait(barrier, 4 + has_up.astype(jnp.int32) + has_down.astype(jnp.int32))

    def remote(src, dst, send, recv, target):
        return pltpu.make_async_remote_copy(
            src_ref=src, dst_ref=dst, send_sem=send, recv_sem=recv, device_id=target, device_id_type=MESH
        )

    keep = pltpu.make_async_copy(blocks, part(rows, rows, layer), local_sem)
    keep.start()

    near_right = remote(own(rows - DIRECT, DIRECT), part(rows - DIRECT, DIRECT, layer), near_send.at[0], near_recv.at[0], right)
    near_left = remote(own(0, DIRECT), part(2 * rows, DIRECT, layer), near_send.at[1], near_recv.at[1], left)

    def along(p, g, direction, src=None):
        first, count = pieces[p]
        return remote(
            part(first, count, g) if src is None else src,
            part(first, count, g),
            z_send.at[p, direction, g],
            z_recv.at[p, g],
            up if direction == 0 else down,
        )

    def start_along(p, g, direction, src=None):
        @pl.when(has_up if direction == 0 else has_down)
        def _():
            along(p, g, direction, src).start()

    for k in range(PIECES):
        src = own(k * step, step)
        start_along(k, layer, 0, src)
        start_along(k, layer, 1, src)

    def far(k, g, from_blocks=False):
        first, count = cut(k, DIRECT, rows - DIRECT)
        src = own(first, count) if from_blocks else part(rows + first, count, g)
        return remote(src, part(odd * 2 * rows + first, count, g), far_send.at[k, g], far_recv.at[k, g], partner)

    def on(k, g, parity):
        first, count = cut(k, *(before if parity else after))
        if not count:
            return None
        return remote(
            part((0 if parity else 2 * rows) + first, count, g),
            part((2 * rows if parity else 0) + first, count, g),
            on_send.at[k, g],
            on_recv.at[k, g],
            beyond,
        )

    def pass_on(k, g):
        far(k, g).wait_recv()
        for parity in (0, 1):
            copy = on(k, g, parity)
            if copy is not None:
                pl.when(odd == parity)(copy.start)

    for k in range(PIECES):
        far(k, layer, True).start()
    near_right.start()
    near_left.start()

    def at_hop(hop, act):
        @pl.when(layer >= hop)
        def _():
            act(layer - hop, 0)

        @pl.when(layer + hop < layers)
        def _():
            act(layer + hop, 1)

    def forward(p, hop):
        def act(g, direction):
            along(p, g, direction).wait_recv()
            start_along(p, g, direction)
            if p < PIECES:
                far(p, g).start()

        at_hop(hop, act)

    edges = (PIECES, PIECES + 1)
    for hop in range(1, layers):
        for k in range(PIECES):
            forward(k, hop)
            if k == PIECES - 1 and hop > 1:
                for p in edges:
                    forward(p, hop - 1)
            if hop == 1:
                pass_on(k, layer)
            else:
                at_hop(hop - 1, lambda g, direction: pass_on(k, g))
        if hop == 1:
            near_right.wait_recv()
            near_left.wait_recv()
            for p in edges:
                start_along(p, layer, 0)
                start_along(p, layer, 1)
    for k in range(PIECES):
        at_hop(layers - 1, lambda g, direction: pass_on(k, g))
    for p in edges:
        forward(p, layers - 1)

    for g in range(layers):
        for k in range(PIECES):
            far(k, g).wait_send()
            for parity in (0, 1):
                copy = on(k, g, parity)
                if copy is not None:
                    pl.when(odd == parity)(copy.wait)
    near_right.wait_send()
    near_left.wait_send()
    for p in range(PIECES + 2):
        for g in range(layers):
            @pl.when(has_up & (layer >= g))
            def _():
                along(p, g, 0).wait_send()

            @pl.when(has_down & (layer <= g))
            def _():
                along(p, g, 1).wait_send()

    keep.wait()


def gather_rows(blocks, shape):
    rows, slots = blocks.shape[:2]
    layers = shape[2]
    return pl.pallas_call(
        functools.partial(gather_kernel, shape),
        out_shape=jax.ShapeDtypeStruct((3 * rows, slots * layers) + blocks.shape[2:], blocks.dtype),
        in_specs=[pl.BlockSpec(memory_space=pl.ANY)],
        out_specs=pl.BlockSpec(memory_space=pl.ANY),
        scratch_shapes=[
            pltpu.SemaphoreType.DMA,
            pltpu.SemaphoreType.DMA((2,)),
            pltpu.SemaphoreType.DMA((2,)),
            pltpu.SemaphoreType.DMA((PIECES, layers)),
            pltpu.SemaphoreType.DMA((PIECES, layers)),
            pltpu.SemaphoreType.DMA((PIECES, layers)),
            pltpu.SemaphoreType.DMA((PIECES, layers)),
            pltpu.SemaphoreType.DMA((PIECES + 2, 2, layers)),
            pltpu.SemaphoreType.DMA((PIECES + 2, layers)),
        ],
        compiler_params=pltpu.CompilerParams(collective_id=0, has_side_effects=True),
    )(blocks)


def multiply_kernel(picked, full, out, held, sems):
    row = pl.program_id(0)
    spare = full.shape[0] // 3 - REACH
    outer, slots = full.shape[0] - 2 * spare, full.shape[1]
    wanted = out.shape[1]

    def fetch(r):
        return pltpu.make_async_copy(full.at[spare + r], held.at[pl.ds(r * slots, slots)], sems.at[r])

    @pl.when(row == 0)
    def _():
        @pl.loop(0, outer)
        def _(r):
            fetch(r).start()

        held[outer * slots] = jnp.zeros(held.shape[1:], held.dtype)

        @pl.loop(0, 2 * REACH)
        def _(r):
            fetch(r).wait()

    fetch(row + 2 * REACH).wait()

    mine = (row + REACH) * slots
    lhs = jnp.concatenate([held[mine + t] for t in range(slots)], axis=1)
    for s in range(0, wanted, 2):
        pair = range(s, min(s + 2, wanted))
        rhs = jnp.concatenate(
            [
                jnp.concatenate([held[picked[row, k * slots + t]] for k in pair], axis=1)
                for t in range(slots)
            ],
            axis=0,
        )
        sums = jnp.dot(lhs, rhs, preferred_element_type=jnp.float32).astype(out.dtype)
        for n, k in enumerate(pair):
            out[0, k] = sums[:, n * out.shape[3] : (n + 1) * out.shape[3]]


def multiply(full, picked, rows, wanted):
    slots, size = full.shape[1:3]
    outer = rows + 2 * REACH
    return pl.pallas_call(
        multiply_kernel,
        out_shape=jax.ShapeDtypeStruct((rows, wanted, size, size), full.dtype),
        grid_spec=pltpu.PrefetchScalarGridSpec(
            num_scalar_prefetch=1,
            grid=(rows,),
            in_specs=[pl.BlockSpec(memory_space=pl.ANY)],
            out_specs=pl.BlockSpec((1, wanted, size, size), lambda i, picked: (i, 0, 0, 0)),
            scratch_shapes=[
                pltpu.VMEM((outer * slots + 1, size, size), full.dtype),
                pltpu.SemaphoreType.DMA((outer,)),
            ],
        ),
        compiler_params=pltpu.CompilerParams(
            dimension_semantics=("arbitrary",), vmem_limit_bytes=48 * 2**20
        ),
    )(picked, full)


def per_device(shape, blocks, pattern, out_pattern):
    rows, wanted = blocks.shape[:2]
    total, slots = pattern.shape
    outer = rows + 2 * REACH
    first = lax.axis_index(("row", "col")) * rows
    full = gather_rows(blocks, shape)
    own_cols = lax.dynamic_slice_in_dim(pattern, first, rows, 0)
    own_out = lax.dynamic_slice(out_pattern, (first, lax.axis_index("layer") * wanted), (rows, wanted))
    where = (own_cols - (first - REACH)) % total
    right_cols = jnp.take(pattern, own_cols, axis=0)
    match = right_cols[:, None, :, :] == own_out[:, :, None, None]
    slot = jnp.max(jnp.where(match, jnp.arange(1, slots + 1, dtype=jnp.int32), 0), axis=-1)
    picked = jnp.where(slot > 0, where[:, None, :] * slots + slot - 1, outer * slots)
    return multiply(full, picked.reshape(rows, wanted * slots), rows, wanted)


def solution(mesh):
    shape = tuple(mesh.shape[axis] for axis in ("row", "col", "layer"))
    spec = P(("row", "col"), "layer", None, None)
    return jax.shard_map(
        functools.partial(per_device, shape),
        mesh=mesh,
        in_specs=(spec, P(), P()),
        out_specs=spec,
        check_vma=False,
    )
```
